256 devices in a mesh: seq: 16 (over z_hi, x), tp: 16 (over z_lo, y, core).
Axes of the slice: x: 4, y: 4, z: 8 (z_hi: 4, z_lo: 2; z = z_hi * 2 + z_lo), core: 2. Of those that a mesh axis runs over, the one named last changes fastest.
Arguments:
- teacher_attn: bfloat16 [2048, 16384], P('seq', 'tp'), may hold values from -6 to 6
- teacher_out_w: bfloat16 [16384, 16384], P('tp', 'seq'), may hold values from -0.046875 to 0.046875
- teacher_resid: bfloat16 [2048, 16384], P(None, 'seq')
- teacher_gain: float32 [16384], P('seq'), may hold values from 0.1 to 1.9
- projector: bfloat16 [16384, 8192], P('seq', 'tp'), may hold values from -0.046875 to 0.046875
- student_attn: bfloat16 [2048, 8192], P('tp', 'seq'), may hold values from -6 to 6
- student_out_w: bfloat16 [8192, 8192], P('seq', 'tp'), may hold values from -0.0625 to 0.0625
- student_resid: bfloat16 [2048, 8192], P('seq', 'tp')
Outputs:
- mse: float32 [], replicated
- grad_student_w: float32 [8192, 8192], P('seq', 'tp')
- grad_projector: float32 [16384, 8192], P('seq', 'tp')
The draws below stay inside these ranges and needn't reach their ends.
All inputs are finite; a program needn't handle non-finite values.
Results may differ from the reference program's by a relative error of at most 0.025.
Values may be sent and summed in bfloat16 or wider, within the bound.
A program may use at most 64 MiB of HBM per device.

```python
import jax
import jax.numpy as jnp
from jax import lax

DT = 16384
DS = 8192
TOKENS = 2048
N_SEQ = 16
N_TP = 16


def draw_teacher_resid(key, part):
    key = jax.random.fold_in(key, 11)
    key_base, key_rough, key_rows = jax.random.split(key, 3)
    columns = jnp.arange(DT, dtype=jnp.float32) / DT
    rough = jax.random.uniform(key_rough, (1, DT), jnp.float32, 0.5, 1.5)
    base = jax.random.normal(key_base, (TOKENS, DT), jnp.float32)
    row_scale = 10.0 ** jax.random.uniform(key_rows, (TOKENS, 1), jnp.float32, -0.5, 0.5)
    column_scale = 10.0 ** (columns - 0.5)
    values = base * row_scale * column_scale[None, :] * rough
    return values.astype(jnp.bfloat16)


def draw_student_resid(key, part):
    key = jax.random.fold_in(key, 13)
    key_base, key_rows, key_columns = jax.random.split(key, 3)
    positions = jnp.arange(TOKENS, dtype=jnp.float32)[:, None] / TOKENS
    row_rough = jax.random.uniform(key_rows, (TOKENS, 1), jnp.float32, 0.5, 1.5)
    column_rough = jax.random.uniform(key_columns, (1, DS), jnp.float32, 0.5, 1.5)
    base = jax.random.normal(key_base, (TOKENS, DS), jnp.float32)
    rising = 10.0 ** (0.5 * positions - 0.25)
    return (base * rising * row_rough * column_rough).astype(jnp.bfloat16)


def raised(drawn, stream_key, source, target, blocks, factor):
    owner, partner = [(jnp.arange(drawn.shape[axis_at]) // (drawn.shape[axis_at] // blocks)).reshape([-1 if axis == axis_at else 1 for axis in range(drawn.ndim)]) for axis_at in (source, target)]
    chosen = jax.random.permutation(stream_key, blocks)[partner]
    strong = (owner == chosen) | (owner == (partner + blocks // 2) % blocks)
    return jnp.where(strong, factor * drawn, drawn)


def level_of(rng, dims, cuts, least, top_value):
    def one(axis_at, shards_of):
        heights = jax.random.uniform(jax.random.fold_in(jax.random.fold_in(rng, 6), axis_at), (shards_of,), jnp.float32, least / len(cuts), top_value / len(cuts))
        return jnp.repeat(jnp.exp(heights), dims[axis_at] // shards_of).reshape((-1,) + (1,) * (len(dims) - axis_at - 1))

    factor_of = one(*cuts[0])
    for cut in cuts[1:]:
        factor_of = factor_of * one(*cut)
    return factor_of


def bell_draw(own_key, shape, scale, bound, cuts=(), kind=jnp.bfloat16):
    factor_of = level_of(own_key, shape, cuts, -0.22, 0.18) if cuts else 1.0
    values = jax.random.normal(own_key, shape, jnp.float32) * scale * factor_of
    return jnp.minimum(jnp.maximum(values, -bound), bound).astype(kind)


def heavy_noise(own_key, shape, spread, limit, pieces, heavy, kind=jnp.bfloat16):
    values = spread * jax.random.normal(own_key, shape, jnp.float32)
    if pieces:
        values = values * level_of(own_key, shape, pieces, -0.22, 0.18)
    return jnp.clip(raised(values, jax.random.fold_in(own_key, 3), *heavy), -limit, limit).astype(kind)


def setup_inputs(seed: int = 0) -> dict:
    splits = jax.random.split(jax.random.key(seed), 9)
    return {
        "teacher_attn": heavy_noise(splits[0], (TOKENS, DT), 1.0, 6.0, ((0, 16), (1, 16)), (1, 0, 16, 2.0)),
        "teacher_out_w": bell_draw(splits[1], (DT, DT), DT ** -0.5, 0.046875, ((0, 16), (1, 16))),
        "teacher_resid": draw_teacher_resid(jax.random.fold_in(splits[8], 71), 0),
        "teacher_gain": jnp.clip(1.0 + 0.18 * jax.random.normal(splits[3], (DT,), jnp.float32), 0.1, 1.9),
        "projector": bell_draw(splits[4], (DT, DS), DT ** -0.5, 0.046875, ((0, 16), (1, 16))),
        "student_attn": heavy_noise(splits[5], (TOKENS, DS), 1.0, 6.0, ((0, 16), (1, 16)), (1, 0, 16, 2.0)),
        "student_out_w": bell_draw(splits[6], (DS, DS), DS ** -0.5, 0.0625, ((0, 16), (1, 16))),
        "student_resid": draw_student_resid(jax.random.fold_in(splits[8], 71), 0),
    }


epsilon = 1e-05
loss_scale = 32.0

def blocked_product(left_matrix, right_matrix, blocks):
    inner = left_matrix.shape[1] // blocks

    def add_block(running, block_index):
        offset = (block_index * inner).astype(jnp.int32)
        left_part = lax.dynamic_slice_in_dim(left_matrix, offset, inner, 1)
        right_part = lax.dynamic_slice_in_dim(right_matrix, offset, inner, 0)
        rounded = jnp.dot(left_part, right_part, preferred_element_type=jnp.float32).astype(jnp.bfloat16)
        rounded = lax.optimization_barrier(rounded)
        return (running + rounded.astype(jnp.float32), None)
    start_sum = jnp.zeros((left_matrix.shape[0], right_matrix.shape[1]), jnp.float32)
    result, _ = lax.scan(add_block, start_sum, jnp.arange(blocks, dtype=jnp.int32))
    return result

def reference(teacher_attn, teacher_out_w, teacher_resid, teacher_gain, projector, student_attn, student_out_w, student_resid):
    teacher_sum = blocked_product(teacher_attn, teacher_out_w, N_TP)
    teacher_hidden = (teacher_resid.astype(jnp.float32) + teacher_sum).astype(jnp.bfloat16)
    hidden_wide = teacher_hidden.astype(jnp.float32)
    squares = lax.optimization_barrier(jnp.sum(hidden_wide * hidden_wide, axis=1, keepdims=True))
    inv_rms = lax.rsqrt(squares / DT + epsilon)
    normed = (hidden_wide * inv_rms * teacher_gain[None, :]).astype(jnp.bfloat16)
    target = blocked_product(normed, projector, N_SEQ)
    student_proj = blocked_product(student_attn, student_out_w, N_SEQ)
    residual_gap = student_resid.astype(jnp.float32) + student_proj - target
    mse = jnp.sum(residual_gap * residual_gap) / (TOKENS * DS)
    error = (loss_scale / TOKENS * residual_gap).astype(jnp.bfloat16)
    grad_student_w = jnp.dot(student_attn.T, error, preferred_element_type=jnp.float32)
    grad_projector = -jnp.dot(normed.T, error, preferred_element_type=jnp.float32)
    return (mse, grad_student_w, grad_projector)
```

```python
import functools

import jax
import jax.numpy as jnp
from jax import lax
from jax.experimental import pallas as pl
from jax.experimental.pallas import tpu as pltpu
from jax.sharding import PartitionSpec as P

MESH = pl.DeviceIdType.MESH
BF = jnp.bfloat16
F32 = jnp.float32

DT = 16384
DS = 8192
EPSILON = 1e-05
LOSS_SCALE = 32.0

NC = 4
ROWS = 128
R = ROWS // NC
TOKENS = 2048
KT = 1024
KS = 512
TILE = 256

PER_CHUNK = {
    "az": 3, "ax": 2, "af": 2,
    "tc": 1, "ty": 3, "tz": 1,
    "pz": 3, "px": 3,
    "nz": 1, "ny": 3, "nf": 3, "nc": 1,
    "gx": 2, "gf": 2, "gz": 3,
    "ez": 3, "ex": 2, "ef": 2,
}
ONCE = {"sz": 1, "sy": 3, "sf": 3, "sc": 1, "mz": 3, "mx": 3, "my": 3, "ml": 1, "mc": 1}
BASE = {}
TOTAL = 0
for _name, _count in PER_CHUNK.items():
    BASE[_name] = TOTAL
    TOTAL += _count * NC
for _name, _count in ONCE.items():
    BASE[_name] = TOTAL
    TOTAL += _count
LOADS = 9


def schedule():
    stages = 18
    order = []
    for tick in range(stages + NC):
        for chunk in range(NC):
            if 0 <= tick - chunk < stages:
                order.append(chunk)
    return order


def kernel(
    ta, w1_hbm, tr, gain_hbm, pj_hbm, sa_hbm, sw_hbm, sr_hbm,
    mse_ref, gs, gp,
    w1, pj, sw, gain, res, sr,
    a_all, cs, cr, own1, qs, yr, own2, zs, zr, hid, psa, psz, psx,
    n_all, s_all, g_part, xr1, xr2, e_wide, es, er, e_all,
    ms, mz, mx, my, ml, mc,
    send, recv, load,
):
    s = lax.axis_index("seq")
    t = lax.axis_index("tp")
    zh, x = s // 4, s % 4
    zl, y, co = t // 8, (t // 2) % 4, t % 2
    zlp, cop = 1 - zl, 1 - co

    def at(zh_, x_, zl_, y_, co_):
        return (zh_ * 4 + x_, zl_ * 8 + y_ * 2 + co_)

    def zh_dev(d):
        return at((zh + d) % 4, x, zl, y, co)

    def x_dev(d):
        return at(zh, (x + d) % 4, zl, y, co)

    def y_dev(d):
        return at(zh, x, zl, (y + d) % 4, co)

    zl_dev = at(zh, x, zlp, y, co)
    co_dev = at(zh, x, zl, y, cop)

    started = []

    def index_of(name, c, i):
        return BASE[name] + (c * PER_CHUNK[name] if name in PER_CHUNK else 0) + i

    def push(name, c, i, src, dst, dev):
        k = index_of(name, c, i)
        copy = pltpu.make_async_remote_copy(
            src_ref=src, dst_ref=dst, send_sem=send.at[k], recv_sem=recv.at[k],
            device_id=dev, device_id_type=MESH,
        )
        copy.start()
        started.append(copy)

    def landed(name, c, i, where):
        k = index_of(name, c, i)
        pltpu.make_async_remote_copy(
            src_ref=where, dst_ref=where, send_sem=send.at[k], recv_sem=recv.at[k],
            device_id=co_dev, device_id_type=MESH,
        ).wait_recv()

    loads = []

    def fetch(src, dst):
        copy = pltpu.make_async_copy(src, dst, load.at[len(loads)])
        copy.start()
        loads.append(copy)
        return copy

    def ax_at(c, z_, x_):
        return a_all.at[c, z_, x_ // 2, x_ % 2]

    own_a = fetch(ta, a_all.at[:, zh, x // 2, x % 2])
    own_s = fetch(sa_hbm, s_all.at[:, zl, y, co])
    get_w1 = fetch(w1_hbm, w1)
    get_res = fetch(tr.at[t], res)
    get_gain = fetch(gain_hbm, gain)
    get_sw = fetch(sw_hbm, sw)
    get_pj = fetch(pj_hbm, pj)
    get_sr = fetch(sr_hbm, sr)

    barrier = pltpu.get_barrier_semaphore()
    peers = [zh_dev(d) for d in (1, 2, 3)] + [x_dev(d) for d in (1, 2, 3)]
    peers += [y_dev(d) for d in (1, 2, 3)] + [zl_dev, co_dev]
    for dev in peers:
        pl.semaphore_signal(barrier, inc=1, device_id=dev, device_id_type=MESH)
    pl.semaphore_wait(barrier, len(peers))

    row = lax.broadcasted_iota(jnp.int32, (R, 128), 0)
    lane = lax.broadcasted_iota(jnp.int32, (R, 128), 1)
    diagonal = row == lane

    low, high = pl.ds(0, 2), pl.ds(2, 2)
    xp, xm, xo = (x + 1) % 4, (x + 3) % 4, (x + 2) % 4

    def student_gather():
        for d in (1, 2, 3):
            push("sy", 0, d - 1, sa_hbm, s_all.at[:, zl, y, co], y_dev(d))
        push("sz", 0, 0, sa_hbm, s_all.at[:, zl, y, co], zl_dev)
        yield
        landed("sz", 0, 0, s_all.at[:, zlp, y, co])
        for d in (1, 2, 3):
            push("sf", 0, d - 1, s_all.at[:, zlp, y, co], s_all.at[:, zlp, y, co], y_dev(d))
        yield
        own_s.wait()
        for d in (1, 2, 3):
            y_ = (y + 4 - d) % 4
            landed("sy", 0, d - 1, s_all.at[:, zl, y_, co])
            landed("sf", 0, d - 1, s_all.at[:, zlp, y_, co])
        push("sc", 0, 0, s_all.at[:, :, :, co], s_all.at[:, :, :, co], co_dev)
        yield
        landed("sc", 0, 0, s_all.at[:, :, :, cop])
        yield

    def chunk(c):
        for d in (1, 3, 2):
            push("az", c, d - 1, ta.at[c], ax_at(c, zh, x), zh_dev(d))
        yield
        if c == 0:
            own_a.wait()
        for d in (1, 3, 2):
            landed("az", c, d - 1, ax_at(c, (zh + 4 - d) % 4, x))
        mine = ax_at(c, slice(None), x)
        push("ax", c, 0, mine, mine, x_dev(1))
        push("ax", c, 1, mine, mine, x_dev(3))
        yield
        landed("ax", c, 0, ax_at(c, slice(None), xm))
        far = ax_at(c, low, xm)
        push("af", c, 0, far, far, x_dev(1))
        landed("ax", c, 1, ax_at(c, slice(None), xp))
        far = ax_at(c, high, xp)
        push("af", c, 1, far, far, x_dev(3))
        yield
        landed("af", c, 0, ax_at(c, low, xo))
        landed("af", c, 1, ax_at(c, high, xo))
        if c == 0:
            get_w1.wait()

        other = a_all[c, :, :, cop].reshape(8 * R, KT)
        for n in range(KT // TILE):
            cols = pl.ds(n * TILE, TILE)
            part = jnp.dot(other, w1[:, cols], preferred_element_type=F32)
            cs[c, :, :, cols] = part.astype(BF).reshape(8, R, TILE)
        push("tc", c, 0, cs.at[c], cr.at[c], co_dev)
        own = a_all[c, :, :, co].reshape(8 * R, KT)
        for n in range(KT // TILE):
            cols = pl.ds(n * TILE, TILE)
            part = jnp.dot(own, w1[:, cols], preferred_element_type=F32)
            own1[c, :, :, cols] = part.reshape(8, R, TILE)
        yield
        landed("tc", c, 0, cr.at[c])
        for k in range(8):
            both = own1[c, k] + cr[c, k].astype(F32)
            own1[c, k] = both
            qs[c, k // 4, k % 4] = both.astype(BF)
        for d in (1, 3, 2):
            push("ty", c, d - 1, qs.at[c, :, (y + d) % 4], yr.at[c, d - 1], y_dev(d))
        yield
        for d in (1, 3, 2):
            landed("ty", c, d - 1, yr.at[c, d - 1])
        theirs = own1[c, zlp * 4 + y]
        for d in (0, 1, 2):
            theirs = theirs + yr[c, d, zlp].astype(F32)
        zs[c] = theirs.astype(BF)
        push("tz", c, 0, zs.at[c], zr.at[c], zl_dev)
        mine = own1[c, zl * 4 + y]
        for d in (0, 1, 2):
            mine = mine + yr[c, d, zl].astype(F32)
        own2[c] = mine
        yield
        landed("tz", c, 0, zr.at[c])
        if c == 0:
            get_res.wait()
            get_gain.wait()
        total = own2[c] + zr[c].astype(F32)
        hidden = (res[c].astype(F32) + total).astype(BF)
        hid[c] = hidden
        wide = hidden.astype(F32)
        squares = jnp.sum(wide * wide, axis=1, keepdims=True)
        line = jnp.sum(jnp.where(diagonal, squares, 0.0), axis=0, keepdims=True)
        psz[c, zh] = jnp.broadcast_to(line, (8, 128))
        for d in (1, 3, 2):
            push("pz", c, d - 1, psz.at[c, zh], psz.at[c, zh], zh_dev(d))
        yield
        for d in (1, 3, 2):
            landed("pz", c, d - 1, psz.at[c, (zh + 4 - d) % 4])
        psx[c, x] = psz[c, 0] + psz[c, 1] + psz[c, 2] + psz[c, 3]
        for d in (1, 3, 2):
            push("px", c, d - 1, psx.at[c, x], psx.at[c, x], x_dev(d))
        yield
        for d in (1, 3, 2):
            landed("px", c, d - 1, psx.at[c, (x + 4 - d) % 4])
        line = psx[c, 0] + psx[c, 1] + psx[c, 2] + psx[c, 3]
        line = jnp.broadcast_to(line[0:1, :], (R, 128))
        squares = jnp.sum(jnp.where(diagonal, line, 0.0), axis=1, keepdims=True)
        inv_rms = lax.rsqrt(squares / DT + EPSILON)
        n_all[c, zl, y, co] = (hid[c].astype(F32) * inv_rms * gain[...]).astype(BF)
        block = n_all.at[c, zl, y, co]
        push("nz", c, 0, block, block, zl_dev)
        for d in (1, 3, 2):
            push("ny", c, d - 1, block, block, y_dev(d))
        yield
        block = n_all.at[c, zlp, y, co]
        landed("nz", c, 0, block)
        for d in (1, 3, 2):
            push("nf", c, d - 1, block, block, y_dev(d))
        yield
        for d in (1, 3, 2):
            landed("ny", c, d - 1, n_all.at[c, zl, (y + 4 - d) % 4, co])
        for d in (1, 3, 2):
            landed("nf", c, d - 1, n_all.at[c, zlp, (y + 4 - d) % 4, co])
        block = n_all.at[c, :, :, co]
        push("nc", c, 0, block, block, co_dev)
        yield
        landed("nc", c, 0, n_all.at[c, :, :, cop])
        if c == 0:
            get_pj.wait()
            get_sw.wait()
        for n in range(KS // TILE):
            cols = pl.ds(n * TILE, TILE)
            for m in range(2):
                half = n_all[c, m].reshape(8 * R, KT)
                s_half = s_all[c, m].reshape(8 * R, KS)
                part = jnp.dot(s_half, sw[:, cols], preferred_element_type=F32)
                part = part - jnp.dot(half, pj[:, cols], preferred_element_type=F32)
                g_part[c, pl.ds(m * 2, 2), :, :, cols] = part.astype(BF).reshape(2, 4, R, TILE)
        push("gx", c, 0, g_part.at[c, low, xo], xr1.at[c, 0], x_dev(1))
        push("gx", c, 1, g_part.at[c, high, xo], xr1.at[c, 1], x_dev(3))
        yield
        landed("gx", c, 0, xr1.at[c, 0])
        for k in range(2):
            g_part[c, k, xp] = (g_part[c, k, xp].astype(F32) + xr1[c, 0, k].astype(F32)).astype(BF)
        push("gf", c, 0, g_part.at[c, :, xp], xr2.at[c, 0], x_dev(1))
        landed("gx", c, 1, xr1.at[c, 1])
        for k in range(2):
            g_part[c, 2 + k, xm] = (
                g_part[c, 2 + k, xm].astype(F32) + xr1[c, 1, k].astype(F32)
            ).astype(BF)
        push("gf", c, 1, g_part.at[c, :, xm], xr2.at[c, 1], x_dev(3))
        yield
        landed("gf", c, 0, xr2.at[c, 0])
        landed("gf", c, 1, xr2.at[c, 1])
        for k in range(4):
            both = g_part[c, k, x].astype(F32) + xr2[c, 0, k].astype(F32) + xr2[c, 1, k].astype(F32)
            e_wide[c, k] = both
            es[c, k] = both.astype(BF)
        for d in (1, 3, 2):
            push("gz", c, d - 1, es.at[c, (zh + d) % 4], er.at[c, d - 1], zh_dev(d))
        yield
        for d in (1, 3, 2):
            landed("gz", c, d - 1, er.at[c, d - 1])
        if c == 0:
            get_sr.wait()
        gap = e_wide[c, zh]
        for d in range(3):
            gap = gap + er[c, d].astype(F32)
        gap = gap + sr[c].astype(F32)
        squared = jnp.sum((gap * gap).reshape(R // 8, 8, KS), axis=0)
        squared = sum(squared[:, 128 * k : 128 * (k + 1)] for k in range(KS // 128))
        if c == 0:
            ms[...] = squared
        else:
            ms[...] += squared
        e_all[c, zh, x] = (LOSS_SCALE / TOKENS * gap).astype(BF)
        block = e_all.at[c, zh, x]
        for d in (1, 3, 2):
            push("ez", c, d - 1, block, block, zh_dev(d))
        yield
        for d in (1, 3, 2):
            landed("ez", c, d - 1, e_all.at[c, (zh + 4 - d) % 4, x])
        block = e_all.at[c, :, x]
        push("ex", c, 0, block, block, x_dev(1))
        push("ex", c, 1, block, block, x_dev(3))
        yield
        landed("ex", c, 0, e_all.at[c, :, xm])
        far = e_all.at[c, low, xm]
        push("ef", c, 0, far, far, x_dev(1))
        landed("ex", c, 1, e_all.at[c, :, xp])
        far = e_all.at[c, high, xp]
        push("ef", c, 1, far, far, x_dev(3))
        yield
        landed("ef", c, 0, e_all.at[c, low, xo])
        landed("ef", c, 1, e_all.at[c, high, xo])
        error = e_all[c].reshape(16 * R, KS)
        over_rows = (((0,), (0,)), ((), ()))
        for m in range(KS // TILE):
            cols = pl.ds(m * TILE, TILE)
            left = s_all[c, :, :, :, :, cols].reshape(16 * R, TILE)
            part = lax.dot_general(left, error, over_rows, preferred_element_type=F32)
            gs[cols, :] = part if c == 0 else gs[cols, :] + part
        for m in range(KT // TILE):
            cols = pl.ds(m * TILE, TILE)
            left = n_all[c, :, :, :, :, cols].reshape(16 * R, TILE)
            part = lax.dot_general(left, error, over_rows, preferred_element_type=F32)
            gp[cols, :] = -part if c == 0 else gp[cols, :] - part
        yield

    def squared_total():
        mz[zh] = ms[...]
        for d in (1, 2, 3):
            push("mz", 0, d - 1, mz.at[zh], mz.at[zh], zh_dev(d))
        yield
        for d in (1, 2, 3):
            landed("mz", 0, d - 1, mz.at[(zh + 4 - d) % 4])
        mx[x] = mz[0] + mz[1] + mz[2] + mz[3]
        for d in (1, 2, 3):
            push("mx", 0, d - 1, mx.at[x], mx.at[x], x_dev(d))
        yield
        for d in (1, 2, 3):
            landed("mx", 0, d - 1, mx.at[(x + 4 - d) % 4])
        my[y] = mx[0] + mx[1] + mx[2] + mx[3]
        for d in (1, 2, 3):
            push("my", 0, d - 1, my.at[y], my.at[y], y_dev(d))
        yield
        for d in (1, 2, 3):
            landed("my", 0, d - 1, my.at[(y + 4 - d) % 4])
        ml[zl] = my[0] + my[1] + my[2] + my[3]
        push("ml", 0, 0, ml.at[zl], ml.at[zl], zl_dev)
        yield
        landed("ml", 0, 0, ml.at[zlp])
        mc[co] = ml[0] + ml[1]
        push("mc", 0, 0, mc.at[co], mc.at[co], co_dev)
        yield
        landed("mc", 0, 0, mc.at[cop])
        mse_ref[0, 0] = jnp.sum(mc[0] + mc[1]) / (TOKENS * DS)
        yield

    chunks = [chunk(c) for c in range(NC)]
    done = [0] * NC
    gather = student_gather()
    total = squared_total()
    for c in schedule():
        next(chunks[c])
        if c == 0 and done[0] in (0, 2, 5, 10):
            next(gather)
        if c == NC - 1 and done[c] >= 14:
            next(total)
        done[c] += 1
    for _ in total:
        pass
    for copy in started:
        copy.wait_send()


def body(teacher_attn, teacher_out_w, teacher_resid, teacher_gain, projector, student_attn, student_out_w, student_resid):
    any_spec = pl.BlockSpec(memory_space=pl.ANY)
    vmem = pltpu.VMEM
    mse, student_grad, projector_grad = pl.pallas_call(
        kernel,
        name="distill",
        out_shape=(
            jax.ShapeDtypeStruct((1, 1), F32),
            jax.ShapeDtypeStruct((KS, KS), F32),
            jax.ShapeDtypeStruct((KT, KS), F32),
        ),
        in_specs=[any_spec] * 8,
        out_specs=(
            pl.BlockSpec(memory_space=pltpu.SMEM),
            pl.BlockSpec(memory_space=vmem),
            pl.BlockSpec(memory_space=vmem),
        ),
        scratch_shapes=[
            vmem((KT, KT), BF),
            vmem((KT, KS), BF),
            vmem((KS, KS), BF),
            vmem((1, KT), F32),
            vmem((NC, R, KT), BF),
            vmem((NC, R, KS), BF),
            vmem((NC, 4, 2, 2, R, KT), BF),
            vmem((NC, 8, R, KT), BF),
            vmem((NC, 8, R, KT), BF),
            vmem((NC, 8, R, KT), F32),
            vmem((NC, 2, 4, R, KT), BF),
            vmem((NC, 3, 2, R, KT), BF),
            vmem((NC, R, KT), F32),
            vmem((NC, R, KT), BF),
            vmem((NC, R, KT), BF),
            vmem((NC, R, KT), BF),
            vmem((8, 128), F32),
            vmem((NC, 4, 8, 128), F32),
            vmem((NC, 4, 8, 128), F32),
            vmem((NC, 2, 4, 2, R, KT), BF),
            vmem((NC, 2, 4, 2, R, KS), BF),
            vmem((NC, 4, 4, R, KS), BF),
            vmem((NC, 2, 2, R, KS), BF),
            vmem((NC, 2, 4, R, KS), BF),
            vmem((NC, 4, R, KS), F32),
            vmem((NC, 4, R, KS), BF),
            vmem((NC, 3, R, KS), BF),
            vmem((NC, 4, 4, R, KS), BF),
            vmem((8, 128), F32),
            vmem((4, 8, 128), F32),
            vmem((4, 8, 128), F32),
            vmem((4, 8, 128), F32),
            vmem((2, 8, 128), F32),
            vmem((2, 8, 128), F32),
            pltpu.SemaphoreType.DMA((TOTAL,)),
            pltpu.SemaphoreType.DMA((TOTAL,)),
            pltpu.SemaphoreType.DMA((LOADS,)),
        ],
        compiler_params=pltpu.CompilerParams(
            collective_id=1, has_side_effects=True, vmem_limit_bytes=60 * 1024 * 1024
        ),
    )(
        teacher_attn.reshape(NC, R, KT),
        teacher_out_w,
        teacher_resid.reshape(16, NC, R, KT),
        teacher_gain.reshape(1, KT),
        projector,
        student_attn.reshape(NC, R, KS),
        student_out_w,
        student_resid.reshape(NC, R, KS),
    )
    return (mse.reshape(()), student_grad, projector_grad)


def solution(mesh):
    in_specs = (
        P("seq", "tp"),
        P("tp", "seq"),
        P(None, "seq"),
        P("seq"),
        P("seq", "tp"),
        P("tp", "seq"),
        P("seq", "tp"),
        P("seq", "tp"),
    )
    out_specs = (P(), P("seq", "tp"), P("seq", "tp"))
    return jax.shard_map(body, mesh=mesh, in_specs=in_specs, out_specs=out_specs, check_vma=False)
```

```python
import functools

import jax
import jax.numpy as jnp
from jax import lax
from jax.experimental import pallas as pl
from jax.experimental.pallas import tpu as pltpu
from jax.sharding import PartitionSpec as P

MESH = pl.DeviceIdType.MESH
BF = jnp.bfloat16
F32 = jnp.float32

DT = 16384
DS = 8192
EPSILON = 1e-05
LOSS_SCALE = 32.0

SIZES = (16, 16, 16, 16, 16, 16, 16, 16)
NC = len(SIZES)
STARTS = tuple(sum(SIZES[:c]) for c in range(NC))
ROWS = 128
TOKENS = 2048
KT = 1024
KS = 512
TILE = 256
GAP_STAGE = 14

PER_CHUNK = {
    "az": 3, "ao": 2, "ag": 2, "ax": 2, "af": 2,
    "tc": 1, "ty": 3, "tz": 1,
    "pz": 3, "px": 3, "iy": 3, "ic": 1,
    "ny": 3, "nc": 1,
    "gx": 3, "gz": 3,
    "ez": 3, "ex": 3,
}
ONCE = {"sz": 1, "sy": 3, "sf": 3, "sc": 1, "mz": 3, "mx": 3, "my": 3, "ml": 1, "mc": 1}
BASE = {}
TOTAL = 0
for _name, _count in PER_CHUNK.items():
    BASE[_name] = TOTAL
    TOTAL += _count * NC
for _name, _count in ONCE.items():
    BASE[_name] = TOTAL
    TOTAL += _count
LOADS = 9

ORDER = (
    0, 1, 1, 0, 0, 2, 0, 1, 3, 2, 0, 2, 4, 0, 1, 3, 3, 5, 2, 4, 1, 0, 4, 6, 1, 3, 5, 5, 7, 2, 0, 2,
    6, 4, 1, 3, 6, 3, 5, 7, 7, 1, 4, 0, 2, 6, 4, 5, 1, 3, 5, 7, 2, 0, 0, 3, 1, 1, 6, 2, 4, 7, 3, 5,
    6, 2, 7, 4, 0, 2, 3, 5, 0, 1, 3, 4, 1, 2, 5, 6, 7, 0, 2, 6, 1, 3, 4, 4, 5, 7, 3, 0, 1, 2, 4, 5,
    5, 6, 7, 4, 5, 1, 3, 6, 0, 2, 6, 7, 7, 4, 6, 6, 2, 3, 7, 5, 4, 7, 1, 3, 5, 6, 0, 2, 7, 5, 6, 4,
    3, 7, 6, 5, 7, 4, 6, 7,
)
GATHER_AT = (0, 2, 5, 11)


def kernel(
    ta, w1_hbm, tr, gain_hbm, pj_hbm, sa_hbm, sw_hbm, sr_hbm,
    mse_ref, gs, gp,
    w1, pj, sw, gain, res, sr,
    a_all, cs, cr, own1, qs, yr, zs, zr, psz, psx, inv_all,
    h_all, n_all, s_all, g_part, xr, e_wide, es, er, e_all,
    ms, mz, mx, my, ml, mc,
    send, recv, load,
):
    s = lax.axis_index("seq")
    t = lax.axis_index("tp")
    zh, x = s // 4, s % 4
    zl, y, co = t // 8, (t // 2) % 4, t % 2
    zlp, cop = 1 - zl, 1 - co

    def at(zh_, x_, zl_, y_, co_):
        return (zh_ * 4 + x_, zl_ * 8 + y_ * 2 + co_)

    def zh_dev(d):
        return at((zh + d) % 4, x, zl, y, co)

    def x_dev(d):
        return at(zh, (x + d) % 4, zl, y, co)

    def y_dev(d):
        return at(zh, x, zl, (y + d) % 4, co)

    zl_dev = at(zh, x, zlp, y, co)
    co_dev = at(zh, x, zl, y, cop)

    started = []

    def index_of(name, c, i):
        return BASE[name] + (c * PER_CHUNK[name] if name in PER_CHUNK else 0) + i

    def push(name, c, i, src, dst, dev):
        k = index_of(name, c, i)
        copy = pltpu.make_async_remote_copy(
            src_ref=src, dst_ref=dst, send_sem=send.at[k], recv_sem=recv.at[k],
            device_id=dev, device_id_type=MESH,
        )
        copy.start()
        started.append(copy)

    def landed(name, c, i, where):
        k = index_of(name, c, i)
        pltpu.make_async_remote_copy(
            src_ref=where, dst_ref=where, send_sem=send.at[k], recv_sem=recv.at[k],
            device_id=co_dev, device_id_type=MESH,
        ).wait_recv()

    loads = []
    waited = set()

    def ready(*copies):
        for copy in copies:
            if id(copy) not in waited:
                waited.add(id(copy))
                copy.wait()

    def fetch(src, dst):
        copy = pltpu.make_async_copy(src, dst, load.at[len(loads)])
        copy.start()
        loads.append(copy)
        return copy

    def rows(c):
        return pl.ds(STARTS[c], SIZES[c])

    def a_at(c, d, x_, cols=slice(None)):
        return a_all.at[d, x_ // 2, x_ % 2, rows(c), cols]

    own_a = fetch(ta, a_all.at[0, x // 2, x % 2])
    own_s = fetch(sa_hbm, s_all.at[zl, y, co])
    get_w1 = fetch(w1_hbm, w1)
    get_res = fetch(tr.at[:, y * 2 + co], res)
    get_gain = fetch(gain_hbm, gain)
    get_sw = fetch(sw_hbm, sw)
    get_pj = fetch(pj_hbm, pj)
    get_sr = fetch(sr_hbm, sr)

    barrier = pltpu.get_barrier_semaphore()
    peers = [zh_dev(d) for d in (1, 2, 3)] + [x_dev(d) for d in (1, 2, 3)]
    peers += [y_dev(d) for d in (1, 2, 3)] + [zl_dev, co_dev]
    for dev in peers:
        pl.semaphore_signal(barrier, inc=1, device_id=dev, device_id_type=MESH)
    pl.semaphore_wait(barrier, len(peers))

    tile_row = lax.broadcasted_iota(jnp.int32, (8, 128), 0)

    def diagonal(c):
        shape = (SIZES[c], 128)
        return lax.broadcasted_iota(jnp.int32, shape, 0) == lax.broadcasted_iota(jnp.int32, shape, 1)


    xp, xm, xo = (x + 1) % 4, (x + 3) % 4, (x + 2) % 4

    def student_gather():
        for d in (1, 2, 3):
            push("sy", 0, d - 1, sa_hbm, s_all.at[zl, y, co], y_dev(d))
        push("sz", 0, 0, sa_hbm, s_all.at[zl, y, co], zl_dev)
        yield
        landed("sz", 0, 0, s_all.at[zlp, y, co])
        for d in (1, 2, 3):
            push("sf", 0, d - 1, s_all.at[zlp, y, co], s_all.at[zlp, y, co], y_dev(d))
        yield
        ready(own_s)
        for d in (1, 2, 3):
            y_ = (y + 4 - d) % 4
            landed("sy", 0, d - 1, s_all.at[zl, y_, co])
            landed("sf", 0, d - 1, s_all.at[zlp, y_, co])
        push("sc", 0, 0, s_all.at[:, :, co], s_all.at[:, :, co], co_dev)
        yield
        landed("sc", 0, 0, s_all.at[:, :, cop])
        yield

    def chunk(c):
        size = SIZES[c]
        at_c = rows(c)
        left_cols, right_cols = pl.ds(0, KT // 2), pl.ds(KT // 2, KT // 2)
        rest = pl.ds(1, 3)
        source = ta.at[at_c]
        for d in (1, 3, 2):
            push("az", c, d - 1, source, a_at(c, d, x), zh_dev(d))
        push("ao", c, 0, source, a_at(c, 0, x), x_dev(1))
        push("ao", c, 1, source, a_at(c, 0, x), x_dev(3))
        yield
        landed("ao", c, 0, a_at(c, 0, xm))
        far = a_at(c, 0, xm, left_cols)
        push("ag", c, 0, far, far, x_dev(1))
        landed("ao", c, 1, a_at(c, 0, xp))
        far = a_at(c, 0, xp, right_cols)
        push("ag", c, 1, far, far, x_dev(3))
        yield
        for d in (1, 3, 2):
            landed("az", c, d - 1, a_at(c, d, x))
        push("ax", c, 0, a_at(c, rest, x), a_at(c, rest, x), x_dev(1))
        push("ax", c, 1, a_at(c, rest, x), a_at(c, rest, x), x_dev(3))
        yield
        landed("ax", c, 0, a_at(c, rest, xm))
        far = a_at(c, rest, xm, left_cols)
        push("af", c, 0, far, far, x_dev(1))
        landed("ax", c, 1, a_at(c, rest, xp))
        far = a_at(c, rest, xp, right_cols)
        push("af", c, 1, far, far, x_dev(3))
        yield
        landed("ag", c, 0, a_at(c, 0, xo, left_cols))
        landed("ag", c, 1, a_at(c, 0, xo, right_cols))
        landed("af", c, 0, a_at(c, rest, xo, left_cols))
        landed("af", c, 1, a_at(c, rest, xo, right_cols))
        ready(own_a, get_w1)

        def z_places(d):
            return pl.ds((zh + 4 - d) % 4 * 2, 2)

        other = a_all[:, :, cop, at_c, :].reshape(8 * size, KT)
        for n in range(KT // TILE):
            cols = pl.ds(n * TILE, TILE)
            part = jnp.dot(other, w1[:, cols], preferred_element_type=F32)
            part = part.astype(BF).reshape(4, 2, size, TILE)
            for d in range(4):
                cs[z_places(d), at_c, cols] = part[d]
        push("tc", c, 0, cs.at[:, at_c], cr.at[:, at_c], co_dev)
        own = a_all[:, :, co, at_c, :].reshape(8 * size, KT)
        for n in range(KT // TILE):
            cols = pl.ds(n * TILE, TILE)
            part = jnp.dot(own, w1[:, cols], preferred_element_type=F32)
            part = part.reshape(4, 2, size, TILE)
            for d in range(4):
                own1[z_places(d), at_c, cols] = part[d]
        yield
        landed("tc", c, 0, cr.at[:, at_c])
        for k in range(8):
            both = own1[k, at_c] + cr[k, at_c].astype(F32)
            own1[k, at_c] = both
            qs[k // 4, k % 4, at_c] = both.astype(BF)
        for d in (1, 3, 2):
            push("ty", c, d - 1, qs.at[:, (y + d) % 4, at_c], yr.at[d - 1, :, at_c], y_dev(d))
        yield
        for d in (1, 3, 2):
            landed("ty", c, d - 1, yr.at[d - 1, :, at_c])
        for k in range(2):
            both = own1[k * 4 + y, at_c]
            for d in range(3):
                both = both + yr[d, k, at_c].astype(F32)
            zs[k, at_c] = both.astype(BF)
        push("tz", c, 0, zs.at[:, at_c], zr.at[:, at_c], zl_dev)
        yield
        landed("tz", c, 0, zr.at[:, at_c])
        ready(get_res)
        lines = []
        for k in range(2):
            total = zs[k, at_c].astype(F32) + zr[k, at_c].astype(F32)
            hidden = (res[k, at_c].astype(F32) + total).astype(BF)
            h_all[k, y, co, at_c] = hidden
            wide = hidden.astype(F32)
            squares = jnp.sum(wide * wide, axis=1, keepdims=True)
            lines.append(jnp.sum(jnp.where(diagonal(c), squares, 0.0), axis=0, keepdims=True))
        psz[c, zh] = jnp.where(tile_row == 0, lines[0], jnp.where(tile_row == 1, lines[1], 0.0))
        for d in (1, 3, 2):
            push("pz", c, d - 1, psz.at[c, zh], psz.at[c, zh], zh_dev(d))
        block = h_all.at[:, y, co, at_c]
        for d in (1, 3, 2):
            push("ny", c, d - 1, block, block, y_dev(d))
        yield
        for d in (1, 3, 2):
            landed("pz", c, d - 1, psz.at[c, (zh + 4 - d) % 4])
        psx[c, x] = psz[c, 0] + psz[c, 1] + psz[c, 2] + psz[c, 3]
        for d in (1, 3, 2):
            push("px", c, d - 1, psx.at[c, x], psx.at[c, x], x_dev(d))
        yield
        for d in (1, 3, 2):
            landed("px", c, d - 1, psx.at[c, (x + 4 - d) % 4])
        line = psx[c, 0] + psx[c, 1] + psx[c, 2] + psx[c, 3]
        inv_all[c, y, co] = lax.rsqrt(line / DT + EPSILON)
        block = inv_all.at[c, y, co]
        for d in (1, 3, 2):
            push("iy", c, d - 1, block, block, y_dev(d))
        yield
        for d in (1, 3, 2):
            landed("ny", c, d - 1, h_all.at[:, (y + 4 - d) % 4, co, at_c])
        block = h_all.at[:, :, co, at_c]
        push("nc", c, 0, block, block, co_dev)
        yield
        for d in (1, 3, 2):
            landed("iy", c, d - 1, inv_all.at[c, (y + 4 - d) % 4, co])
        block = inv_all.at[c, :, co]
        push("ic", c, 0, block, block, co_dev)
        yield
        landed("nc", c, 0, h_all.at[:, :, cop, at_c])
        landed("ic", c, 0, inv_all.at[c, :, cop])
        ready(get_gain, get_pj, get_sw)
        for _ in gather:
            pass

        def norm(k, carry):
            for core in range(2):
                inv = inv_all[c, k, core]
                for z_ in range(2):
                    line = jnp.broadcast_to(inv[z_ : z_ + 1, :], (size, 128))
                    column = jnp.sum(jnp.where(diagonal(c), line, 0.0), axis=1, keepdims=True)
                    wide = h_all[z_, k, core, at_c].astype(F32)
                    n_all[z_, k, core, at_c] = (wide * column * gain[...]).astype(BF)
            return carry

        lax.fori_loop(0, 4, norm, 0)
        for m in range(2):
            half = n_all[m, :, :, at_c, :].reshape(8 * size, KT)
            s_half = s_all[m, :, :, at_c, :].reshape(8 * size, KS)
            for n in range(KS // TILE):
                cols = pl.ds(n * TILE, TILE)
                part = jnp.dot(s_half, sw[:, cols], preferred_element_type=F32)
                part = part - jnp.dot(half, pj[:, cols], preferred_element_type=F32)
                g_part[pl.ds(m * 2, 2), :, at_c, cols] = part.astype(BF).reshape(2, 4, size, TILE)
        for d in (1, 3, 2):
            push("gx", c, d - 1, g_part.at[:, (x + d) % 4, at_c], xr.at[d - 1, :, at_c], x_dev(d))
        yield
        for d in (1, 3, 2):
            landed("gx", c, d - 1, xr.at[d - 1, :, at_c])
        for k in range(4):
            both = g_part[k, x, at_c].astype(F32)
            for d in range(3):
                both = both + xr[d, k, at_c].astype(F32)
            e_wide[k, at_c] = both
            es[k, at_c] = both.astype(BF)
        for d in (1, 3, 2):
            push("gz", c, d - 1, es.at[(zh + d) % 4, at_c], er.at[d - 1, at_c], zh_dev(d))
        yield
        for d in (1, 3, 2):
            landed("gz", c, d - 1, er.at[d - 1, at_c])
        ready(get_sr)
        gap = e_wide[zh, at_c]
        for d in range(3):
            gap = gap + er[d, at_c].astype(F32)
        gap = gap + sr[at_c].astype(F32)
        squared = jnp.sum((gap * gap).reshape(size // 8, 8, KS), axis=0)
        ms[c] = sum(squared[:, 128 * k : 128 * (k + 1)] for k in range(KS // 128))
        if c == final:
            next(mse_steps)
        e_all[zh, x, at_c] = (LOSS_SCALE / TOKENS * gap).astype(BF)
        block = e_all.at[zh, x, at_c]
        for d in (1, 3, 2):
            push("ez", c, d - 1, block, block, zh_dev(d))
        yield
        if c == final:
            next(mse_steps)
            next(mse_steps)
        for d in (1, 3, 2):
            landed("ez", c, d - 1, e_all.at[(zh + 4 - d) % 4, x, at_c])
        block = e_all.at[:, x, at_c]
        for d in (1, 3, 2):
            push("ex", c, d - 1, block, block, x_dev(d))
        if c == final:
            next(mse_steps)
        yield
        for d in (1, 3, 2):
            landed("ex", c, d - 1, e_all.at[:, (x + 4 - d) % 4, at_c])
        if c == final:
            next(mse_steps)
        error = e_all[:, :, at_c, :].reshape(16 * size, KS)
        over_rows = (((0,), (0,)), ((), ()))
        for m in range(KS // TILE):
            cols = pl.ds(m * TILE, TILE)
            left = s_all[:, :, :, at_c, cols].reshape(16 * size, TILE)
            part = lax.dot_general(left, error, over_rows, preferred_element_type=F32)
            gs[cols, :] = part if first_grad[0] else gs[cols, :] + part
        for m in range(KT // TILE):
            cols = pl.ds(m * TILE, TILE)
            left = n_all[:, :, :, at_c, cols].reshape(16 * size, TILE)
            part = lax.dot_general(left, error, over_rows, preferred_element_type=F32)
            gp[cols, :] = -part if first_grad[0] else gp[cols, :] - part
        first_grad[0] = False
        yield

    def squared_total():
        my[y] = sum(ms[c] for c in range(NC))
        for d in (1, 2, 3):
            push("my", 0, d - 1, my.at[y], my.at[y], y_dev(d))
        yield
        for d in (1, 2, 3):
            landed("my", 0, d - 1, my.at[(y + 4 - d) % 4])
        ml[zl] = my[0] + my[1] + my[2] + my[3]
        push("ml", 0, 0, ml.at[zl], ml.at[zl], zl_dev)
        yield
        landed("ml", 0, 0, ml.at[zlp])
        mc[co] = ml[0] + ml[1]
        push("mc", 0, 0, mc.at[co], mc.at[co], co_dev)
        yield
        landed("mc", 0, 0, mc.at[cop])
        mz[zh] = mc[0] + mc[1]
        for d in (1, 3, 2):
            push("mz", 0, d - 1, mz.at[zh], mz.at[zh], zh_dev(d))
        yield
        for d in (1, 2, 3):
            landed("mz", 0, d - 1, mz.at[(zh + 4 - d) % 4])
        mx[x] = mz[0] + mz[1] + mz[2] + mz[3]
        for d in (1, 2, 3):
            push("mx", 0, d - 1, mx.at[x], mx.at[x], x_dev(d))
        yield
        for d in (1, 2, 3):
            landed("mx", 0, d - 1, mx.at[(x + 4 - d) % 4])
        mse_ref[0, 0] = jnp.sum(mx[0] + mx[1] + mx[2] + mx[3]) / (TOKENS * DS)
        yield

    first_grad = [True]
    seen = [0] * NC
    for c in ORDER:
        if seen[c] == GAP_STAGE:
            final = c
        seen[c] += 1
    chunks = [chunk(c) for c in range(NC)]
    done = [0] * NC
    gather = student_gather()
    mse_steps = squared_total()
    for c in ORDER:
        next(chunks[c])
        if c == 0 and done[0] in GATHER_AT:
            next(gather, None)
        done[c] += 1
    for _ in mse_steps:
        pass
    for copy in started:
        copy.wait_send()


def body(teacher_attn, teacher_out_w, teacher_resid, teacher_gain, projector, student_attn, student_out_w, student_resid):
    any_spec = pl.BlockSpec(memory_space=pl.ANY)
    vmem = pltpu.VMEM
    mse, student_grad, projector_grad = pl.pallas_call(
        kernel,
        name="distill",
        out_shape=(
            jax.ShapeDtypeStruct((1, 1), F32),
            jax.ShapeDtypeStruct((KS, KS), F32),
            jax.ShapeDtypeStruct((KT, KS), F32),
        ),
        in_specs=[any_spec] * 8,
        out_specs=(
            pl.BlockSpec(memory_space=pltpu.SMEM),
            pl.BlockSpec(memory_space=vmem),
            pl.BlockSpec(memory_space=vmem),
        ),
        scratch_shapes=[
            vmem((KT, KT), BF),
            vmem((KT, KS), BF),
            vmem((KS, KS), BF),
            vmem((1, KT), F32),
            vmem((2, ROWS, KT), BF),
            vmem((ROWS, KS), BF),
            vmem((4, 2, 2, ROWS, KT), BF),
            vmem((8, ROWS, KT), BF),
            vmem((8, ROWS, KT), BF),
            vmem((8, ROWS, KT), F32),
            vmem((2, 4, ROWS, KT), BF),
            vmem((3, 2, ROWS, KT), BF),
            vmem((2, ROWS, KT), BF),
            vmem((2, ROWS, KT), BF),
            vmem((NC, 4, 8, 128), F32),
            vmem((NC, 4, 8, 128), F32),
            vmem((NC, 4, 2, 8, 128), F32),
            vmem((2, 4, 2, ROWS, KT), BF),
            vmem((2, 4, 2, ROWS, KT), BF),
            vmem((2, 4, 2, ROWS, KS), BF),
            vmem((4, 4, ROWS, KS), BF),
            vmem((3, 4, ROWS, KS), BF),
            vmem((4, ROWS, KS), F32),
            vmem((4, ROWS, KS), BF),
            vmem((3, ROWS, KS), BF),
            vmem((4, 4, ROWS, KS), BF),
            vmem((NC, 8, 128), F32),
            vmem((4, 8, 128), F32),
            vmem((4, 8, 128), F32),
            vmem((4, 8, 128), F32),
            vmem((2, 8, 128), F32),
            vmem((2, 8, 128), F32),
            pltpu.SemaphoreType.DMA((TOTAL,)),
            pltpu.SemaphoreType.DMA((TOTAL,)),
            pltpu.SemaphoreType.DMA((LOADS,)),
        ],
        compiler_params=pltpu.CompilerParams(
            collective_id=1, has_side_effects=True, vmem_limit_bytes=60 * 1024 * 1024
        ),
    )(
        teacher_attn,
        teacher_out_w,
        teacher_resid.reshape(2, 8, ROWS, KT),
        teacher_gain.reshape(1, KT),
        projector,
        student_attn,
        student_out_w,
        student_resid,
    )
    return (mse.reshape(()), student_grad, projector_grad)


def solution(mesh):
    in_specs = (
        P("seq", "tp"),
        P("tp", "seq"),
        P(None, "seq"),
        P("seq"),
        P("seq", "tp"),
        P("tp", "seq"),
        P("seq", "tp"),
        P("seq", "tp"),
    )
    out_specs = (P(), P("seq", "tp"), P("seq", "tp"))
    return jax.shard_map(body, mesh=mesh, in_specs=in_specs, out_specs=out_specs, check_vma=False)
```

```python
import functools

import jax
import jax.numpy as jnp
from jax import lax
from jax.experimental import pallas as pl
from jax.experimental.pallas import tpu as pltpu
from jax.sharding import PartitionSpec as P

MESH = pl.DeviceIdType.MESH
BF = jnp.bfloat16
F32 = jnp.float32

DT = 16384
DS = 8192
EPSILON = 1e-05
LOSS_SCALE = 32.0

SIZES = (16, 16, 16, 16, 16, 16, 16, 16)
NC = len(SIZES)
STARTS = tuple(sum(SIZES[:c]) for c in range(NC))
ROWS = 128
TOKENS = 2048
KT = 1024
KS = 512
TILE = 256
GAP_STAGE = 14

PER_CHUNK = {
    "az": 3, "ao": 2, "ag": 2, "ax": 2, "af": 2,
    "tc": 1, "ty": 3, "tz": 1,
    "pz": 3, "px": 3, "iy": 3, "ic": 1,
    "ny": 3, "nc": 1,
    "gx": 3, "gz": 3,
    "ez": 3, "ex": 3,
}
ONCE = {"sz": 1, "sy": 3, "sf": 3, "sc": 1, "mz": 3, "mx": 3, "my": 3, "ml": 1, "mc": 1}
BASE = {}
TOTAL = 0
for _name, _count in PER_CHUNK.items():
    BASE[_name] = TOTAL
    TOTAL += _count * NC
for _name, _count in ONCE.items():
    BASE[_name] = TOTAL
    TOTAL += _count
LOADS = 9

ORDER = (
    0, 1, 1, 0, 0, 2, 0, 1, 3, 2, 0, 2, 4, 0, 1, 3, 3, 5, 2, 4, 1, 0, 4, 6, 1, 3, 5, 5, 7, 2, 0, 2,
    6, 4, 1, 3, 6, 3, 5, 7, 7, 1, 4, 0, 2, 6, 4, 5, 1, 3, 5, 7, 2, 0, 0, 3, 1, 1, 6, 2, 4, 7, 3, 5,
    6, 2, 7, 4, 0, 2, 3, 5, 0, 1, 3, 4, 1, 2, 5, 6, 7, 0, 2, 6, 1, 3, 4, 4, 5, 7, 3, 0, 1, 2, 4, 5,
    5, 6, 7, 4, 5, 1, 3, 6, 0, 2, 6, 7, 7, 4, 6, 6, 2, 3, 7, 5, 4, 7, 1, 3, 5, 6, 0, 2, 7, 5, 6, 4,
    3, 7, 6, 5, 7, 4, 6, 7,
)
GATHER_AT = (0, 2, 5, 11)


def kernel(
    ta, w1_hbm, tr, gain_hbm, pj_hbm, sa_hbm, sw_hbm, sr_hbm,
    mse_ref, gs, gp,
    w1, pj, sw, gain, res, sr,
    a_all, cs, cr, own1, qs, yr, zs, zr, psz, psx, inv_all,
    h_all, n_all, s_all, g_part, xr, e_wide, es, er, e_all,
    ms, mz, mx, my, ml, mc,
    send, recv, load,
):
    s = lax.axis_index("seq")
    t = lax.axis_index("tp")
    zh, x = s // 4, s % 4
    zl, y, co = t // 8, (t // 2) % 4, t % 2
    zlp, cop = 1 - zl, 1 - co

    def at(zh_, x_, zl_, y_, co_):
        return (zh_ * 4 + x_, zl_ * 8 + y_ * 2 + co_)

    def zh_dev(d):
        return at((zh + d) % 4, x, zl, y, co)

    def x_dev(d):
        return at(zh, (x + d) % 4, zl, y, co)

    def y_dev(d):
        return at(zh, x, zl, (y + d) % 4, co)

    zl_dev = at(zh, x, zlp, y, co)
    co_dev = at(zh, x, zl, y, cop)

    started = []

    def index_of(name, c, i):
        return BASE[name] + (c * PER_CHUNK[name] if name in PER_CHUNK else 0) + i

    def push(name, c, i, src, dst, dev):
        k = index_of(name, c, i)
        copy = pltpu.make_async_remote_copy(
            src_ref=src, dst_ref=dst, send_sem=send.at[k], recv_sem=recv.at[k],
            device_id=dev, device_id_type=MESH,
        )
        copy.start()
        started.append(copy)

    def landed(name, c, i, where):
        k = index_of(name, c, i)
        pltpu.make_async_remote_copy(
            src_ref=where, dst_ref=where, send_sem=send.at[k], recv_sem=recv.at[k],
            device_id=co_dev, device_id_type=MESH,
        ).wait_recv()

    loads = []
    waited = set()

    def ready(*copies):
        for copy in copies:
            if id(copy) not in waited:
                waited.add(id(copy))
                copy.wait()

    def fetch(src, dst):
        copy = pltpu.make_async_copy(src, dst, load.at[len(loads)])
        copy.start()
        loads.append(copy)
        return copy

    def rows(c):
        return pl.ds(STARTS[c], SIZES[c])

    def a_at(c, d, x_, cols=slice(None)):
        return a_all.at[d, x_ // 2, x_ % 2, rows(c), cols]

    own_a = fetch(ta, a_all.at[0, x // 2, x % 2])
    own_s = fetch(sa_hbm, s_all.at[zl, y, co])
    get_w1 = fetch(w1_hbm, w1)
    get_res = fetch(tr.at[:, y * 2 + co], res)
    get_gain = fetch(gain_hbm, gain)
    get_sw = fetch(sw_hbm, sw)
    get_pj = fetch(pj_hbm, pj)
    get_sr = fetch(sr_hbm, sr)

    barrier = pltpu.get_barrier_semaphore()
    peers = [zh_dev(d) for d in (1, 2, 3)] + [x_dev(d) for d in (1, 2, 3)]
    peers += [y_dev(d) for d in (1, 2, 3)] + [zl_dev, co_dev]
    for dev in peers:
        pl.semaphore_signal(barrier, inc=1, device_id=dev, device_id_type=MESH)
    pl.semaphore_wait(barrier, len(peers))

    tile_row = lax.broadcasted_iota(jnp.int32, (8, 128), 0)

    def diagonal(c):
        shape = (SIZES[c], 128)
        return lax.broadcasted_iota(jnp.int32, shape, 0) == lax.broadcasted_iota(jnp.int32, shape, 1)


    xp, xm, xo = (x + 1) % 4, (x + 3) % 4, (x + 2) % 4

    def student_gather():
        for d in (1, 2, 3):
            push("sy", 0, d - 1, sa_hbm, s_all.at[zl, y, co], y_dev(d))
        push("sz", 0, 0, sa_hbm, s_all.at[zl, y, co], zl_dev)
        yield
        landed("sz", 0, 0, s_all.at[zlp, y, co])
        for d in (1, 2, 3):
            push("sf", 0, d - 1, s_all.at[zlp, y, co], s_all.at[zlp, y, co], y_dev(d))
        yield
        ready(own_s)
        for d in (1, 2, 3):
            y_ = (y + 4 - d) % 4
            landed("sy", 0, d - 1, s_all.at[zl, y_, co])
            landed("sf", 0, d - 1, s_all.at[zlp, y_, co])
        push("sc", 0, 0, s_all.at[:, :, co], s_all.at[:, :, co], co_dev)
        yield
        landed("sc", 0, 0, s_all.at[:, :, cop])
        yield

    def chunk(c):
        size = SIZES[c]
        at_c = rows(c)
        left_cols, right_cols = pl.ds(0, KT // 2), pl.ds(KT // 2, KT // 2)
        rest = pl.ds(1, 3)
        source = ta.at[at_c]
        for d in (1, 3, 2):
            push("az", c, d - 1, source, a_at(c, d, x), zh_dev(d))
        push("ao", c, 0, source, a_at(c, 0, x), x_dev(1))
        push("ao", c, 1, source, a_at(c, 0, x), x_dev(3))
        yield
        landed("ao", c, 0, a_at(c, 0, xm))
        far = a_at(c, 0, xm, left_cols)
        push("ag", c, 0, far, far, x_dev(1))
        landed("ao", c, 1, a_at(c, 0, xp))
        far = a_at(c, 0, xp, right_cols)
        push("ag", c, 1, far, far, x_dev(3))
        yield
        for d in (1, 3, 2):
            landed("az", c, d - 1, a_at(c, d, x))
        push("ax", c, 0, a_at(c, rest, x), a_at(c, rest, x), x_dev(1))
        push("ax", c, 1, a_at(c, rest, x), a_at(c, rest, x), x_dev(3))
        yield
        landed("ax", c, 0, a_at(c, rest, xm))
        far = a_at(c, rest, xm, left_cols)
        push("af", c, 0, far, far, x_dev(1))
        landed("ax", c, 1, a_at(c, rest, xp))
        far = a_at(c, rest, xp, right_cols)
        push("af", c, 1, far, far, x_dev(3))
        yield
        landed("ag", c, 0, a_at(c, 0, xo, left_cols))
        landed("ag", c, 1, a_at(c, 0, xo, right_cols))
        landed("af", c, 0, a_at(c, rest, xo, left_cols))
        landed("af", c, 1, a_at(c, rest, xo, right_cols))
        ready(own_a, get_w1)

        def z_places(d):
            return pl.ds((zh + 4 - d) % 4 * 2, 2)

        other = a_all[:, :, cop, at_c, :].reshape(8 * size, KT)
        for n in range(KT // TILE):
            cols = pl.ds(n * TILE, TILE)
            part = jnp.dot(other, w1[:, cols], preferred_element_type=F32)
            part = part.astype(BF).reshape(4, 2, size, TILE)
            for d in range(4):
                cs[z_places(d), at_c, cols] = part[d]
        push("tc", c, 0, cs.at[:, at_c], cr.at[:, at_c], co_dev)
        own = a_all[:, :, co, at_c, :].reshape(8 * size, KT)
        for n in range(KT // TILE):
            cols = pl.ds(n * TILE, TILE)
            part = jnp.dot(own, w1[:, cols], preferred_element_type=F32)
            part = part.reshape(4, 2, size, TILE)
            for d in range(4):
                own1[z_places(d), at_c, cols] = part[d]
        yield
        landed("tc", c, 0, cr.at[:, at_c])
        for k in range(8):
            both = own1[k, at_c] + cr[k, at_c].astype(F32)
            own1[k, at_c] = both
            qs[k // 4, k % 4, at_c] = both.astype(BF)
        for d in (1, 3, 2):
            push("ty", c, d - 1, qs.at[:, (y + d) % 4, at_c], yr.at[d - 1, :, at_c], y_dev(d))
        yield
        for d in (1, 3, 2):
            landed("ty", c, d - 1, yr.at[d - 1, :, at_c])
        for k in range(2):
            both = own1[k * 4 + y, at_c]
            for d in range(3):
                both = both + yr[d, k, at_c].astype(F32)
            zs[k, at_c] = both.astype(BF)
        push("tz", c, 0, zs.at[:, at_c], zr.at[:, at_c], zl_dev)
        yield
        landed("tz", c, 0, zr.at[:, at_c])
        ready(get_res)
        lines = []
        for k in range(2):
            total = zs[k, at_c].astype(F32) + zr[k, at_c].astype(F32)
            hidden = (res[k, at_c].astype(F32) + total).astype(BF)
            h_all[k, y, co, at_c] = hidden
            wide = hidden.astype(F32)
            squares = jnp.sum(wide * wide, axis=1, keepdims=True)
            lines.append(jnp.sum(jnp.where(diagonal(c), squares, 0.0), axis=0, keepdims=True))
        psz[c, zh] = jnp.where(tile_row == 0, lines[0], jnp.where(tile_row == 1, lines[1], 0.0))
        for d in (1, 3, 2):
            push("pz", c, d - 1, psz.at[c, zh], psz.at[c, zh], zh_dev(d))
        block = h_all.at[:, y, co, at_c]
        for d in (1, 3, 2):
            push("ny", c, d - 1, block, block, y_dev(d))
        yield
        for d in (1, 3, 2):
            landed("pz", c, d - 1, psz.at[c, (zh + 4 - d) % 4])
        psx[c, x] = psz[c, 0] + psz[c, 1] + psz[c, 2] + psz[c, 3]
        for d in (1, 3, 2):
            push("px", c, d - 1, psx.at[c, x], psx.at[c, x], x_dev(d))
        yield
        for d in (1, 3, 2):
            landed("px", c, d - 1, psx.at[c, (x + 4 - d) % 4])
        line = psx[c, 0] + psx[c, 1] + psx[c, 2] + psx[c, 3]
        inv_all[c, y, co] = lax.rsqrt(line / DT + EPSILON)
        block = inv_all.at[c, y, co]
        for d in (1, 3, 2):
            push("iy", c, d - 1, block, block, y_dev(d))
        yield
        for d in (1, 3, 2):
            landed("ny", c, d - 1, h_all.at[:, (y + 4 - d) % 4, co, at_c])
        block = h_all.at[:, :, co, at_c]
        push("nc", c, 0, block, block, co_dev)
        yield
        for d in (1, 3, 2):
            landed("iy", c, d - 1, inv_all.at[c, (y + 4 - d) % 4, co])
        block = inv_all.at[c, :, co]
        push("ic", c, 0, block, block, co_dev)
        yield
        landed("nc", c, 0, h_all.at[:, :, cop, at_c])
        landed("ic", c, 0, inv_all.at[c, :, cop])
        ready(get_gain, get_pj, get_sw)
        for _ in gather:
            pass

        def norm(k, carry):
            for core in range(2):
                inv = inv_all[c, k, core]
                for z_ in range(2):
                    line = jnp.broadcast_to(inv[z_ : z_ + 1, :], (size, 128))
                    column = jnp.sum(jnp.where(diagonal(c), line, 0.0), axis=1, keepdims=True)
                    wide = h_all[z_, k, core, at_c].astype(F32)
                    n_all[z_, k, core, at_c] = (wide * column * gain[...]).astype(BF)
            return carry

        lax.fori_loop(0, 4, norm, 0)
        for m in range(2):
            half = n_all[m, :, :, at_c, :].reshape(8 * size, KT)
            s_half = s_all[m, :, :, at_c, :].reshape(8 * size, KS)
            for n in range(KS // TILE):
                cols = pl.ds(n * TILE, TILE)
                part = jnp.dot(s_half, sw[:, cols], preferred_element_type=F32)
                part = part - jnp.dot(half, pj[:, cols], preferred_element_type=F32)
                g_part[pl.ds(m * 2, 2), :, at_c, cols] = part.astype(BF).reshape(2, 4, size, TILE)
        for d in (1, 3, 2):
            push("gx", c, d - 1, g_part.at[:, (x + d) % 4, at_c], xr.at[d - 1, :, at_c], x_dev(d))
        yield
        for d in (1, 3, 2):
            landed("gx", c, d - 1, xr.at[d - 1, :, at_c])
        for k in range(4):
            both = g_part[k, x, at_c].astype(F32)
            for d in range(3):
                both = both + xr[d, k, at_c].astype(F32)
            e_wide[k, at_c] = both
            es[k, at_c] = both.astype(BF)
        for d in (1, 3, 2):
            push("gz", c, d - 1, es.at[(zh + d) % 4, at_c], er.at[d - 1, at_c], zh_dev(d))
        yield
        for d in (1, 3, 2):
            landed("gz", c, d - 1, er.at[d - 1, at_c])
        ready(get_sr)
        gap = e_wide[zh, at_c]
        for d in range(3):
            gap = gap + er[d, at_c].astype(F32)
        gap = gap + sr[at_c].astype(F32)
        squared = jnp.sum((gap * gap).reshape(size // 8, 8, KS), axis=0)
        ms[c] = sum(squared[:, 128 * k : 128 * (k + 1)] for k in range(KS // 128))
        if c == final:
            next(mse_steps)
        e_all[zh, x, at_c] = (LOSS_SCALE / TOKENS * gap).astype(BF)
        block = e_all.at[zh, x, at_c]
        for d in (1, 3, 2):
            push("ez", c, d - 1, block, block, zh_dev(d))
        yield
        if c == final:
            next(mse_steps)
        for d in (1, 3, 2):
            landed("ez", c, d - 1, e_all.at[(zh + 4 - d) % 4, x, at_c])
        block = e_all.at[:, x, at_c]
        for d in (1, 3, 2):
            push("ex", c, d - 1, block, block, x_dev(d))
        if c == final:
            next(mse_steps)
            next(mse_steps)
        yield
        for d in (1, 3, 2):
            landed("ex", c, d - 1, e_all.at[:, (x + 4 - d) % 4, at_c])
        if c == final:
            next(mse_steps)
        error = e_all[:, :, at_c, :].reshape(16 * size, KS)
        over_rows = (((0,), (0,)), ((), ()))
        for m in range(KS // TILE):
            cols = pl.ds(m * TILE, TILE)
            left = s_all[:, :, :, at_c, cols].reshape(16 * size, TILE)
            part = lax.dot_general(left, error, over_rows, preferred_element_type=F32)
            gs[cols, :] = part if first_grad[0] else gs[cols, :] + part
        for m in range(KT // TILE):
            cols = pl.ds(m * TILE, TILE)
            left = n_all[:, :, :, at_c, cols].reshape(16 * size, TILE)
            part = lax.dot_general(left, error, over_rows, preferred_element_type=F32)
            gp[cols, :] = -part if first_grad[0] else gp[cols, :] - part
        first_grad[0] = False
        yield

    def squared_total():
        my[y] = sum(ms[c] for c in range(NC))
        for d in (1, 2, 3):
            push("my", 0, d - 1, my.at[y], my.at[y], y_dev(d))
        yield
        for d in (1, 2, 3):
            landed("my", 0, d - 1, my.at[(y + 4 - d) % 4])
        ml[zl] = my[0] + my[1] + my[2] + my[3]
        push("ml", 0, 0, ml.at[zl], ml.at[zl], zl_dev)
        yield
        landed("ml", 0, 0, ml.at[zlp])
        mc[co] = ml[0] + ml[1]
        push("mc", 0, 0, mc.at[co], mc.at[co], co_dev)
        yield
        landed("mc", 0, 0, mc.at[cop])
        mz[zh] = mc[0] + mc[1]
        for d in (1, 3, 2):
            push("mz", 0, d - 1, mz.at[zh], mz.at[zh], zh_dev(d))
        yield
        for d in (1, 2, 3):
            landed("mz", 0, d - 1, mz.at[(zh + 4 - d) % 4])
        mx[x] = mz[0] + mz[1] + mz[2] + mz[3]
        for d in (1, 2, 3):
            push("mx", 0, d - 1, mx.at[x], mx.at[x], x_dev(d))
        yield
        for d in (1, 2, 3):
            landed("mx", 0, d - 1, mx.at[(x + 4 - d) % 4])
        mse_ref[0, 0] = jnp.sum(mx[0] + mx[1] + mx[2] + mx[3]) / (TOKENS * DS)
        yield

    first_grad = [True]
    seen = [0] * NC
    for c in ORDER:
        if seen[c] == GAP_STAGE:
            final = c
        seen[c] += 1
    chunks = [chunk(c) for c in range(NC)]
    done = [0] * NC
    gather = student_gather()
    mse_steps = squared_total()
    for c in ORDER:
        next(chunks[c])
        if c == 0 and done[0] in GATHER_AT:
            next(gather, None)
        done[c] += 1
    for _ in mse_steps:
        pass
    for copy in started:
        copy.wait_send()


def body(teacher_attn, teacher_out_w, teacher_resid, teacher_gain, projector, student_attn, student_out_w, student_resid):
    any_spec = pl.BlockSpec(memory_space=pl.ANY)
    vmem = pltpu.VMEM
    mse, student_grad, projector_grad = pl.pallas_call(
        kernel,
        name="distill",
        out_shape=(
            jax.ShapeDtypeStruct((1, 1), F32),
            jax.ShapeDtypeStruct((KS, KS), F32),
            jax.ShapeDtypeStruct((KT, KS), F32),
        ),
        in_specs=[any_spec] * 8,
        out_specs=(
            pl.BlockSpec(memory_space=pltpu.SMEM),
            pl.BlockSpec(memory_space=vmem),
            pl.BlockSpec(memory_space=vmem),
        ),
        scratch_shapes=[
            vmem((KT, KT), BF),
            vmem((KT, KS), BF),
            vmem((KS, KS), BF),
            vmem((1, KT), F32),
            vmem((2, ROWS, KT), BF),
            vmem((ROWS, KS), BF),
            vmem((4, 2, 2, ROWS, KT), BF),
            vmem((8, ROWS, KT), BF),
            vmem((8, ROWS, KT), BF),
            vmem((8, ROWS, KT), F32),
            vmem((2, 4, ROWS, KT), BF),
            vmem((3, 2, ROWS, KT), BF),
            vmem((2, ROWS, KT), BF),
            vmem((2, ROWS, KT), BF),
            vmem((NC, 4, 8, 128), F32),
            vmem((NC, 4, 8, 128), F32),
            vmem((NC, 4, 2, 8, 128), F32),
            vmem((2, 4, 2, ROWS, KT), BF),
            vmem((2, 4, 2, ROWS, KT), BF),
            vmem((2, 4, 2, ROWS, KS), BF),
            vmem((4, 4, ROWS, KS), BF),
            vmem((3, 4, ROWS, KS), BF),
            vmem((4, ROWS, KS), F32),
            vmem((4, ROWS, KS), BF),
            vmem((3, ROWS, KS), BF),
            vmem((4, 4, ROWS, KS), BF),
            vmem((NC, 8, 128), F32),
            vmem((4, 8, 128), F32),
            vmem((4, 8, 128), F32),
            vmem((4, 8, 128), F32),
            vmem((2, 8, 128), F32),
            vmem((2, 8, 128), F32),
            pltpu.SemaphoreType.DMA((TOTAL,)),
            pltpu.SemaphoreType.DMA((TOTAL,)),
            pltpu.SemaphoreType.DMA((LOADS,)),
        ],
        compiler_params=pltpu.CompilerParams(
            collective_id=1, has_side_effects=True, vmem_limit_bytes=60 * 1024 * 1024
        ),
    )(
        teacher_attn,
        teacher_out_w,
        teacher_resid.reshape(2, 8, ROWS, KT),
        teacher_gain.reshape(1, KT),
        projector,
        student_attn,
        student_out_w,
        student_resid,
    )
    return (mse.reshape(()), student_grad, projector_grad)


def solution(mesh):
    in_specs = (
        P("seq", "tp"),
        P("tp", "seq"),
        P(None, "seq"),
        P("seq"),
        P("seq", "tp"),
        P("tp", "seq"),
        P("seq", "tp"),
        P("seq", "tp"),
    )
    out_specs = (P(), P("seq", "tp"), P("seq", "tp"))
    return jax.shard_map(body, mesh=mesh, in_specs=in_specs, out_specs=out_specs, check_vma=False)
```
